512 devices in a mesh: dp: 16 (over z), fsdp: 32 (over x, y, core).
Axes of the slice: x: 4, y: 4, z: 16, core: 2. Of those that a mesh axis runs over, the one named last changes fastest.
Arguments:
- prompt_hidden: bfloat16 [32768, 4096], P(('dp', 'fsdp')), may hold values from -6 to 6
- resp_hidden: bfloat16 [65536, 4096], P(('dp', 'fsdp')), may hold values from -6 to 6
- resp_query: bfloat16 [65536, 2048], P(('dp', 'fsdp')), may hold values from -80 to 80
- ln_gain: float32 [4096], replicated, may hold values from 0.25 to 1.75
- key_gain: float32 [128], replicated, may hold values from 0.1 to 1.9
- w_kv: bfloat16 [4096, 1024], P(('dp', 'fsdp')), may hold values from -0.09375 to 0.09375
- prompt_len: int32 [64], P('dp'), may hold values from 64 to 512, as said below
- resp_len: int32 [512], P(('dp', 'fsdp')), may hold values from 1 to 128, as said below
- owner: int32 [512], P(('dp', 'fsdp')), may hold values from 0 to 3, as said below
Outputs:
- attended: bfloat16 [65536, 2048], P(('dp', 'fsdp'))
The draws below stay inside these ranges and needn't reach their ends.
Inputs may be any that keep to these rules, and one draw needn't show every extreme that they name: `prompt_len`: each group has one prompt of length exactly 512. `resp_len`: each group has one response of length exactly 128. `owner`: in each group every prompt index is named by exactly 8 responses.
All inputs are finite; a program needn't handle non-finite values.
Results may differ from the reference program's by a relative error of at most 0.014.
The reference program's roundings to bfloat16 on the way count: a program that leaves them out, or rounds other values in their place, can miss the bound.
Values may be sent and summed in bfloat16 or wider, within the bound.
A program may use at most 64 MiB of HBM per device.

```python
import jax
import jax.numpy as jnp
from jax import lax

D = 4096
HD = 128
QH = 16
KVH = 4
G = 8
LP = 512
LR = 128
PG = 4
SUB = 16
N_DP = 16
N_FSDP = 32


def draw_prompt_len(key, part):
    key = jax.random.fold_in(key, 11)
    first, second = jax.random.split(key)
    values = jax.random.randint(first, (N_DP, PG), LP // 8, LP + 1)
    picked = jax.random.randint(second, (N_DP, 1), 0, PG)
    values = jnp.where(jnp.arange(PG)[None, :] == picked, LP, values)
    return values.reshape(-1).astype(jnp.int32)


def draw_resp_len(key, part):
    key = jax.random.fold_in(key, 12)
    first, second = jax.random.split(key)
    values = jax.random.randint(first, (N_DP, N_FSDP), 1, LR + 1)
    picked = jax.random.randint(second, (N_DP, 1), 0, N_FSDP)
    values = jnp.where(jnp.arange(N_FSDP)[None, :] == picked, LR, values)
    return values.reshape(-1).astype(jnp.int32)


def draw_owner(key, part):
    key = jax.random.fold_in(key, 13)
    keys = jax.random.split(key, N_DP)
    orders = jax.vmap(lambda single: jax.random.permutation(single, N_FSDP))(keys)
    return (orders // G).reshape(-1).astype(jnp.int32)


def draw_resp_query(key, part):
    key = jax.random.fold_in(key, 14)
    first = jax.random.fold_in(key, 0)
    shape = (N_DP * N_FSDP * LR, QH * HD)
    values = jnp.clip(jax.random.normal(first, shape, jnp.float32), -6.0, 6.0)
    return values.astype(jnp.bfloat16)


def shard_levels(key, extent, cuts, least, top_value):
    factor_of = 1.0
    for axis_at, shards_of in cuts:
        heights = jax.random.uniform(jax.random.fold_in(jax.random.fold_in(key, 6), axis_at), (shards_of,), jnp.float32, least / len(cuts), top_value / len(cuts))
        factor_of = factor_of * jnp.repeat(jnp.exp(heights), extent[axis_at] // shards_of).reshape((-1,) + (1,) * (len(extent) - 1 - axis_at))
    return factor_of


def noise(key, dims, scale, bound, shards=(), kind=jnp.bfloat16):
    drawn = scale * jax.random.normal(key, dims, jnp.float32)
    if shards:
        drawn = drawn * shard_levels(key, dims, shards, -0.22, 0.18)
    return jnp.clip(drawn, -bound, bound).astype(kind)


def setup_inputs(seed: int = 0) -> dict:
    splits = jax.random.split(jax.random.key(seed), 10)
    prompt_hidden = noise(splits[0], (N_DP * PG * LP, D), 1.0, 6.0, ((0, 512),))
    resp_hidden = noise(splits[1], (N_DP * N_FSDP * LR, D), 1.0, 6.0, ((0, 512),))
    resp_query = draw_resp_query(jax.random.fold_in(splits[9], 71), 0)
    ln_gain = jnp.clip(1.0 + 0.15 * jax.random.normal(splits[3], (D,), jnp.float32), 0.25, 1.75)
    key_gain = jnp.clip(1.0 + 0.18 * jax.random.normal(splits[4], (HD,), jnp.float32), 0.1, 1.9)
    w_kv = noise(splits[5], (D, 2 * KVH * HD), D ** -0.5, 0.09375, ((0, 512),))
    prompt_len = draw_prompt_len(jax.random.fold_in(splits[9], 71), 0)
    resp_len = draw_resp_len(jax.random.fold_in(splits[9], 71), 0)
    owner = draw_owner(jax.random.fold_in(splits[9], 71), 0)
    return {"prompt_hidden": prompt_hidden, "resp_hidden": resp_hidden, "resp_query": resp_query, "ln_gain": ln_gain, "key_gain": key_gain, "w_kv": w_kv, "prompt_len": prompt_len, "resp_len": resp_len, "owner": owner}


def rms_scale(values, gain):
    mean_sq = lax.optimization_barrier(jnp.mean(values * values, axis=-1, keepdims=True))
    return values * lax.rsqrt(mean_sq + 1e-06) * gain

def rotate(keys, positions):
    half = HD // 2
    inv_freq = 1000000.0 ** (-(jnp.arange(half, dtype=jnp.float32) * 2.0) / HD)
    angles = positions[:, None] * inv_freq[None, :]
    cosine = jnp.cos(angles)[:, None, :]
    sine = jnp.sin(angles)[:, None, :]
    first = keys[..., :half]
    second = keys[..., half:]
    return jnp.concatenate([first * cosine - second * sine, second * cosine + first * sine], axis=-1)

def project(hidden, ln_gain, key_gain, w_kv, positions):
    normed = rms_scale(hidden.astype(jnp.float32), ln_gain).astype(jnp.bfloat16)
    kv = jnp.dot(normed, w_kv, preferred_element_type=jnp.float32)
    keys = kv[:, :KVH * HD].reshape(-1, KVH, HD)
    keys = rotate(rms_scale(keys, key_gain), positions)
    return jnp.concatenate([keys.reshape(-1, KVH * HD), kv[:, KVH * HD:]], axis=-1).astype(jnp.bfloat16)

def attend(query, prefix, own, plen, rlen):
    width = KVH * HD
    keys = jnp.concatenate([prefix[:, :width], own[:, :width]], axis=0).reshape(LP + LR, KVH, HD)
    vals = jnp.concatenate([prefix[:, width:], own[:, width:]], axis=0).reshape(LP + LR, KVH, HD)
    qry = query.reshape(LR, KVH, QH // KVH, HD)
    scores = jnp.einsum('ighd,khd->hgik', qry.astype(jnp.float32), keys.astype(jnp.float32)) / jnp.sqrt(jnp.float32(HD))
    cols = jnp.arange(LP + LR, dtype=jnp.int32)[None, :]
    rows = jnp.arange(LR, dtype=jnp.int32)[:, None]
    allowed = jnp.where(cols < LP, cols < plen, cols - LP <= rows)
    scores = jnp.where(allowed[None, None], scores, -jnp.inf)
    top = lax.optimization_barrier(jnp.max(scores, axis=-1, keepdims=True))
    expo = jnp.exp(scores - top)
    probs = (expo / lax.optimization_barrier(jnp.sum(expo, axis=-1, keepdims=True))).astype(jnp.bfloat16)
    out = jnp.einsum('hgik,khd->ighd', probs.astype(jnp.float32), vals.astype(jnp.float32))
    out = out.reshape(LR, QH * HD)
    live = jnp.arange(LR, dtype=jnp.int32)[:, None] < rlen
    return jnp.where(live, out, 0.0).astype(jnp.bfloat16)

def reference(prompt_hidden, resp_hidden, resp_query, ln_gain, key_gain, w_kv, prompt_len, resp_len, owner):
    count_prompts = N_DP * PG
    count_resp = N_DP * N_FSDP
    ordered = prompt_hidden.reshape(N_DP, N_FSDP, PG, SUB, D).transpose(0, 2, 1, 3, 4).reshape(count_prompts * LP, D)
    prompt_pos = jnp.tile(jnp.arange(LP, dtype=jnp.float32), count_prompts)
    prompt_cache = project(ordered, ln_gain, key_gain, w_kv, prompt_pos)
    which = jnp.arange(count_resp, dtype=jnp.int32) // N_FSDP * PG + owner
    base = prompt_len[which].astype(jnp.float32)
    resp_pos = (base[:, None] + jnp.arange(LR, dtype=jnp.float32)[None, :]).reshape(-1)
    resp_cache = project(resp_hidden, ln_gain, key_gain, w_kv, resp_pos)
    queries = resp_query.reshape(count_resp, LR, QH * HD)
    owns = resp_cache.reshape(count_resp, LR, 2 * KVH * HD)

    def one(index):
        prompt_index = which[index]
        prefix = lax.dynamic_slice_in_dim(prompt_cache, (prompt_index * LP).astype(jnp.int32), LP, 0)
        return attend(queries[index], prefix, owns[index], prompt_len[prompt_index], resp_len[index])
    result = lax.map(one, jnp.arange(count_resp, dtype=jnp.int32))
    return result.reshape(count_resp * LR, QH * HD)
```

```python
import functools

import jax
import jax.numpy as jnp
import numpy as np
from jax import lax
from jax.experimental import pallas as pl
from jax.experimental.pallas import tpu as pltpu
from jax.sharding import PartitionSpec as P

MESH = pl.DeviceIdType.MESH
NZ, NX, NY = 16, 4, 4
HD = 128
KVH = 4
QPK = 4
LP = 512
LR = 128
PG = 4
SUB = 16
D = 4096
EPS = 1e-06
BIG = -1e30


def place():
    f = lax.axis_index("fsdp")
    return lax.axis_index("dp"), f // 8, (f // 2) % NY, f % 2


def device(z, x, y, c):
    return (z, (x * NY + y) * 2 + c)


def gather_kernel(
    prompt_ref, resp_ref, w_ref, gain_ref, key_gain_ref, freq_ref, len_ref, owner_ref,
    out_ref,
    hid, normed, wall, wrx, wbuf, acc, meta, meta_rx, cos_ref, sin_ref, cache, picked,
    in_sem, ex_send, ex_recv, z_send, z_recv,
    w2_send, w2_recv, w3_send, w3_recv, w4_send, w4_recv,
    p2_send, p2_recv, p3_send, p3_recv, p4_send, p4_recv,
):
    z, x, y, c = place()
    other = 1 - c

    def to_z(d):
        return device((z + d) % NZ, x, y, c)

    def to_x(d):
        return device(z, (x + d) % NX, y, c)

    def to_y(d):
        return device(z, x, (y + d) % NY, c)

    mate = device(z, x, y, other)

    def copy(src, dst, send, recv, to):
        return pltpu.make_async_remote_copy(
            src_ref=src, dst_ref=dst, send_sem=send, recv_sem=recv, device_id=to, device_id_type=MESH
        )

    in_copies = [
        pltpu.make_async_copy(prompt_ref, hid.at[pl.ds(0, PG)], in_sem.at[0]),
        pltpu.make_async_copy(resp_ref, hid.at[pl.ds(PG, 8)], in_sem.at[1]),
    ]
    for cp in in_copies:
        cp.start()

    peers = [mate] + [to_z(d) for d in range(1, NZ)] + [to_x(d) for d in (1, 2, 3)] + [to_y(d) for d in (1, 2, 3)]
    barrier = pltpu.get_barrier_semaphore()
    for peer in peers:
        pl.semaphore_signal(barrier, inc=1, device_id=peer, device_id_type=MESH)

    for kv in range(2):
        for h in range(KVH):
            j = kv * KVH + h
            wall[kv, h] = w_ref[:, j * HD : (j + 1) * HD].astype(jnp.float32)
    owner = owner_ref[0]
    plen = len_ref[owner].astype(jnp.float32)
    line = lax.broadcasted_iota(jnp.int32, (8, HD), 0)
    meta[...] = jnp.where(line == 0, plen, jnp.where(line - 1 == owner, 1.0, 0.0))
    pl.semaphore_wait(barrier, len(peers))

    ex_w = copy(wall.at[:, pl.ds(2 * other, 2)], wrx, ex_send.at[0], ex_recv.at[0], mate)
    ex_w.start()
    ex_m = copy(meta, meta_rx, ex_send.at[1], ex_recv.at[1], mate)
    ex_m.start()
    ex_w.wait_recv()
    for kv in range(2):
        for h in range(2):
            mine = wall[kv, 2 * c + h]
            theirs = wrx[kv, h]
            first = jnp.where(c == 0, mine, theirs)
            second = jnp.where(c == 0, theirs, mine)
            wbuf[2 * kv + h, z, x, y] = jnp.concatenate([first, second], axis=0).astype(jnp.bfloat16)

    def z_copy(d):
        block = wbuf.at[:, z, x, y]
        return copy(block, block, z_send.at[d], z_recv.at[d], to_z(d))

    for d in (1, 15, 2, 14, 3, 13, 4, 12, 5, 11, 6, 10, 7, 9, 8):
        z_copy(d).start()

    for cp in in_copies:
        cp.wait()
    gain = gain_ref[...]

    @pl.loop(0, 12)
    def _(i):
        v = hid[i].astype(jnp.float32)
        scale = lax.rsqrt(jnp.mean(v * v, axis=-1, keepdims=True) + EPS)
        row = jnp.where(i < PG, 2 * i + c, 2 * PG + 8 * c + i - PG)
        normed[row] = (v * scale * gain).astype(jnp.bfloat16)

    ex_n = []
    for p in range(PG):
        rows = normed.at[2 * p + c]
        ex_n.append(copy(rows, rows, ex_send.at[2 + p], ex_recv.at[2 + p], mate))
    rows = normed.at[pl.ds(2 * PG + 8 * c, 8)]
    ex_n.append(copy(rows, rows, ex_send.at[6], ex_recv.at[6], mate))
    for cp in ex_n:
        cp.start()

    ex_m.wait_recv()
    freq = freq_ref[...]
    lane = lax.broadcasted_iota(jnp.int32, (32, HD), 1)
    row = lax.broadcasted_iota(jnp.int32, (32, HD), 0)
    sign = jnp.where(lane < HD // 2, -1.0, 1.0)
    mine, theirs = meta[0:1, :], meta_rx[0:1, :]
    lens = (jnp.where(c == 0, mine, theirs), jnp.where(c == 0, theirs, mine))

    @pl.loop(0, 9)
    def _(i):
        j = i - 1
        base = jnp.where(i == 0, (32 * (x * NY + y)).astype(jnp.float32), jnp.where(j < 4, lens[0], lens[1]))
        off = jnp.where(i == 0, 0, (j % 4) * 32)
        angle = (base + (row + off).astype(jnp.float32)) * freq
        cos_ref[i] = jnp.cos(angle)
        sin_ref[i] = jnp.sin(angle) * sign

    acc[...] = jnp.zeros_like(acc)
    for cp in ex_n:
        cp.wait_recv()

    def order(t):
        step = jnp.where(t % 2 == 1, (t + 1) // 2, (8 - t // 2) % 8)
        return (z // 2 + step) % 8

    def planes(t):
        ph = order(t)
        return 2 * ph, 2 * ph + 1

    def w2_copies(t):
        za, zb = planes(t)
        a, b = wbuf.at[:, za, x, y], wbuf.at[:, zb, x, y]
        out = []
        for d in (1, 3, 2):
            out.append(copy(a, a, w2_send.at[t, d - 1], w2_recv.at[t, d - 1], to_y(d)))
            out.append(copy(b, b, w2_send.at[t, d + 2], w2_recv.at[t, d + 2], to_x(d)))
        return out

    def w3_copies(t):
        za, zb = planes(t)
        a, b = wbuf.at[:, za, x], wbuf.at[:, zb, :, y]
        return [
            copy(a, a, w3_send.at[t, 0], w3_recv.at[t, 0], to_x(1)),
            copy(b, b, w3_send.at[t, 1], w3_recv.at[t, 1], to_y(1)),
            copy(a, a, w3_send.at[t, 2], w3_recv.at[t, 2], to_x(3)),
            copy(b, b, w3_send.at[t, 3], w3_recv.at[t, 3], to_y(3)),
        ]

    def w4_copies(t):
        za, zb = planes(t)
        lo, hi = pl.ds(0, 2), pl.ds(2, 2)
        a0, b0 = wbuf.at[lo, za, (x + 3) % NX], wbuf.at[lo, zb, :, (y + 3) % NY]
        a1, b1 = wbuf.at[hi, za, (x + 1) % NX], wbuf.at[hi, zb, :, (y + 1) % NY]
        return [
            copy(a0, a0, w4_send.at[t, 0], w4_recv.at[t, 0], to_x(1)),
            copy(b0, b0, w4_send.at[t, 1], w4_recv.at[t, 1], to_y(1)),
            copy(a1, a1, w4_send.at[t, 2], w4_recv.at[t, 2], to_x(3)),
            copy(b1, b1, w4_send.at[t, 3], w4_recv.at[t, 3], to_y(3)),
        ]

    def wait_z(plane):
        d = (z - plane + NZ) % NZ
        block = wbuf.at[:, plane, x, y]
        copy(block, block, z_send.at[d], z_recv.at[d], mate).wait_recv()

    @pl.loop(0, 11)
    def _(t):
        @pl.when(jnp.logical_and(t >= 2, t < 10))
        def _():
            s = t - 2
            for cp in w3_copies(s):
                cp.wait_recv()
            for cp in w4_copies(s):
                cp.start()

        @pl.when(jnp.logical_and(t >= 1, t < 9))
        def _():
            s = t - 1
            for cp in w2_copies(s):
                cp.wait_recv()
            for cp in w3_copies(s):
                cp.start()

        @pl.when(t < 8)
        def _():
            za, zb = planes(t)

            @pl.when(za != z)
            def _():
                wait_z(za)

            @pl.when(zb != z)
            def _():
                wait_z(zb)

            for cp in w2_copies(t):
                cp.start()

        @pl.when(t >= 3)
        def _():
            s = t - 3
            for cp in w4_copies(s):
                cp.wait_recv()
            ph = order(s)
            za = 2 * ph
            parts = [wbuf[u, pl.ds(za, 2)].reshape(512, HD) for u in range(4)]
            w = jnp.concatenate(parts, axis=1)
            left = normed[:, :, pl.ds(pl.multiple_of(ph * 512, 512), 512)].reshape(384, 512)
            acc[...] += jnp.dot(left, w, preferred_element_type=jnp.float32)

    key_gain = key_gain_ref[...]

    def finish(kv, h, start, size, cos, sin):
        j = kv * 2 + h
        v = acc[start : start + size, j * HD : (j + 1) * HD]
        if kv == 0:
            v = v * lax.rsqrt(jnp.mean(v * v, axis=-1, keepdims=True) + EPS) * key_gain
            v = v * cos + pltpu.roll(v, HD // 2, 1) * sin
        return v.astype(jnp.bfloat16)

    for h in range(2):
        for kv in range(2):
            for p in range(PG):
                cache[h, kv, p, x, y] = finish(kv, h, p * 32, 32, cos_ref[0], sin_ref[0])

    def p2_copies(p):
        a, b = cache.at[0, :, p, x, y], cache.at[1, :, p, x, y]
        out = []
        for d in (1, 3, 2):
            out.append(copy(a, a, p2_send.at[p, d - 1], p2_recv.at[p, d - 1], to_x(d)))
            out.append(copy(b, b, p2_send.at[p, d + 2], p2_recv.at[p, d + 2], to_y(d)))
        return out

    def p3_copies(p):
        a, b = cache.at[0, :, p, :, y], cache.at[1, :, p, x]
        return [
            copy(a, a, p3_send.at[p, 0], p3_recv.at[p, 0], to_y(1)),
            copy(b, b, p3_send.at[p, 1], p3_recv.at[p, 1], to_x(1)),
            copy(a, a, p3_send.at[p, 2], p3_recv.at[p, 2], to_y(3)),
            copy(b, b, p3_send.at[p, 3], p3_recv.at[p, 3], to_x(3)),
        ]

    def p4_copies(p):
        a0, b0 = cache.at[0, 0, p, :, (y + 3) % NY], cache.at[1, 0, p, (x + 3) % NX]
        a1, b1 = cache.at[0, 1, p, :, (y + 1) % NY], cache.at[1, 1, p, (x + 1) % NX]
        return [
            copy(a0, a0, p4_send.at[p, 0], p4_recv.at[p, 0], to_y(1)),
            copy(b0, b0, p4_send.at[p, 1], p4_recv.at[p, 1], to_x(1)),
            copy(a1, a1, p4_send.at[p, 2], p4_recv.at[p, 2], to_y(3)),
            copy(b1, b1, p4_send.at[p, 3], p4_recv.at[p, 3], to_x(3)),
        ]

    for p in range(PG):
        for cp in p2_copies(p):
            cp.start()

    def resp(kv, h, which):
        cos = cos_ref[pl.ds(1 + 4 * which, 4)].reshape(LR, HD)
        sin = sin_ref[pl.ds(1 + 4 * which, 4)].reshape(LR, HD)
        j = kv * 2 + h
        v = acc[pl.ds(pl.multiple_of(128 + 128 * which, 128), LR), j * HD : (j + 1) * HD]
        if kv == 0:
            v = v * lax.rsqrt(jnp.mean(v * v, axis=-1, keepdims=True) + EPS) * key_gain
            v = v * cos + pltpu.roll(v, HD // 2, 1) * sin
        return v.astype(jnp.bfloat16)

    for h in range(2):
        for kv in range(2):
            picked[kv, h, LP : LP + LR] = resp(kv, h, other)
            out_ref[kv, 2 * c + h, LP : LP + LR] = resp(kv, h, c)

    @pl.loop(0, PG + 2)
    def _(t):
        @pl.when(jnp.logical_and(t >= 1, t < PG + 1))
        def _():
            p = t - 1
            for cp in p3_copies(p):
                cp.wait_recv()
            for cp in p4_copies(p):
                cp.start()

        @pl.when(t < PG)
        def _():
            for cp in p2_copies(t):
                cp.wait_recv()
            for cp in p3_copies(t):
                cp.start()

        @pl.when(t >= 2)
        def _():
            for cp in p4_copies(t - 2):
                cp.wait_recv()

    for h in range(2):
        for kv in range(2):
            total = None
            for p in range(PG):
                weight = meta_rx[1 + p : 2 + p, :].astype(jnp.bfloat16)
                part = cache[h, kv, p].reshape(LP, HD) * weight
                total = part if total is None else total + part
            picked[kv, h, 0:LP] = total
    block = out_ref.at[:, pl.ds(2 * c, 2)]
    ex_o = copy(picked, block, ex_send.at[7], ex_recv.at[7], mate)
    ex_o.start()
    for h in range(2):
        for kv in range(2):
            out_ref[kv, 2 * c + h, 0:LP] = cache[h, kv, owner].reshape(LP, HD)
    ex_o.wait_recv()

    ex_w.wait_send()
    ex_m.wait_send()
    ex_o.wait_send()
    for cp in ex_n:
        cp.wait_send()
    for d in range(1, NZ):
        z_copy(d).wait_send()

    @pl.loop(0, 8)
    def _(t):
        for cp in w2_copies(t) + w3_copies(t) + w4_copies(t):
            cp.wait_send()

    @pl.loop(0, PG)
    def _(p):
        for cp in p2_copies(p) + p3_copies(p) + p4_copies(p):
            cp.wait_send()


def attend_kernel(len_ref, owner_ref, rlen_ref, q_ref, kv_ref, o_ref):
    scale = np.float32(np.log2(np.e) / np.sqrt(HD))
    head = pl.program_id(0)

    def columns(g):
        return pl.ds(pl.multiple_of((g * KVH + head) * HD, HD), HD)

    q = jnp.concatenate([q_ref[:, columns(g)] for g in range(QPK)], axis=0)
    keys, vals = kv_ref[0, 0], kv_ref[1, 0]
    s = lax.dot_general(q, keys, (((1,), (1,)), ((), ())), preferred_element_type=jnp.float32) * scale
    plen = len_ref[owner_ref[0]]
    cols = lax.broadcasted_iota(jnp.int32, (LR, LP + LR), 1)
    rows = lax.broadcasted_iota(jnp.int32, (LR, LP + LR), 0)
    allowed = cols < jnp.where(cols < LP, plen, LP + 1 + rows)
    bias = jnp.where(allowed, 0.0, BIG)
    live = lax.broadcasted_iota(jnp.int32, (LR, HD), 0) < rlen_ref[0]
    for g in range(QPK):
        t = s[g * LR : (g + 1) * LR] + bias
        e = jnp.exp2(t - jnp.max(t, axis=-1, keepdims=True))
        total = jnp.sum(e, axis=-1, keepdims=True)
        out = jnp.dot(e.astype(jnp.bfloat16), vals, preferred_element_type=jnp.float32) / total
        o_ref[:, columns(g)] = jnp.where(live, out, 0.0).astype(jnp.bfloat16)


def body(
    prompt_hidden, resp_hidden, resp_query, ln_gain, key_gain, w_kv, prompt_len, resp_len, owner
):
    half = HD // 2
    inv = np.float32(1000000.0) ** (-(np.arange(half, dtype=np.float32) * np.float32(2.0)) / np.float32(HD))
    freq = jnp.asarray(np.concatenate([inv, inv])[None, :].astype(np.float32))
    vmem = pl.BlockSpec(memory_space=pltpu.VMEM)
    smem = pl.BlockSpec(memory_space=pltpu.SMEM)
    anym = pl.BlockSpec(memory_space=pl.ANY)
    bf, f32 = jnp.bfloat16, jnp.float32
    dma = pltpu.SemaphoreType.DMA
    kv = pl.pallas_call(
        gather_kernel,
        name="project_and_share",
        out_shape=jax.ShapeDtypeStruct((2, KVH, LP + LR, HD), bf),
        in_specs=[anym, anym, vmem, vmem, vmem, vmem, smem, smem],
        out_specs=vmem,
        scratch_shapes=[
            pltpu.VMEM((12, SUB, D), bf),
            pltpu.VMEM((24, SUB, D), bf),
            pltpu.VMEM((2, KVH, 8, HD), f32),
            pltpu.VMEM((2, 2, 8, HD), f32),
            pltpu.VMEM((4, NZ, NX, NY, SUB, HD), bf),
            pltpu.VMEM((384, 512), f32),
            pltpu.VMEM((8, HD), f32),
            pltpu.VMEM((8, HD), f32),
            pltpu.VMEM((9, 32, HD), f32),
            pltpu.VMEM((9, 32, HD), f32),
            pltpu.VMEM((2, 2, PG, NX, NY, 32, HD), bf),
            pltpu.VMEM((2, 2, LP + LR, HD), bf),
            dma((2,)), dma((8,)), dma((8,)), dma((NZ,)), dma((NZ,)),
            dma((8, 6)), dma((8, 6)), dma((8, 4)), dma((8, 4)), dma((8, 4)), dma((8, 4)),
            dma((PG, 6)), dma((PG, 6)), dma((PG, 4)), dma((PG, 4)), dma((PG, 4)), dma((PG, 4)),
        ],
        compiler_params=pltpu.CompilerParams(
            collective_id=0, has_side_effects=True, vmem_limit_bytes=48 << 20
        ),
    )(
        prompt_hidden.reshape(PG, SUB, D), resp_hidden.reshape(8, SUB, D), w_kv,
        ln_gain.reshape(1, D), key_gain.reshape(1, HD), freq, prompt_len, owner,
    )
    return pl.pallas_call(
        attend_kernel,
        name="attend",
        out_shape=jax.ShapeDtypeStruct((LR, KVH * QPK * HD), bf),
        grid=(KVH,),
        in_specs=[
            smem, smem, smem,
            pl.BlockSpec((LR, KVH * QPK * HD), lambda h: (0, 0)),
            pl.BlockSpec((2, 1, LP + LR, HD), lambda h: (0, h, 0, 0)),
        ],
        out_specs=pl.BlockSpec((LR, KVH * QPK * HD), lambda h: (0, 0)),
        compiler_params=pltpu.CompilerParams(vmem_limit_bytes=32 << 20),
    )(prompt_len, owner, resp_len, resp_query, kv)


def solution(mesh):
    in_specs = (
        P(("dp", "fsdp"), None),
        P(("dp", "fsdp"), None),
        P(("dp", "fsdp"), None),
        P(),
        P(),
        P(("dp", "fsdp"), None),
        P("dp"),
        P(("dp", "fsdp")),
        P(("dp", "fsdp")),
    )
    out_specs = P(("dp", "fsdp"), None)
    return jax.shard_map(body, mesh=mesh, in_specs=in_specs, out_specs=out_specs, check_vma=False)
```

```python
import functools

import jax
import jax.numpy as jnp
import numpy as np
from jax import lax
from jax.experimental import pallas as pl
from jax.experimental.pallas import tpu as pltpu
from jax.sharding import PartitionSpec as P

MESH = pl.DeviceIdType.MESH
NZ, NX, NY = 16, 4, 4
HD = 128
KVH = 4
QPK = 4
LP = 512
LR = 128
PG = 4
SUB = 16
D = 4096
EPS = 1e-06
BIG = -1e30
LAG = 2


def place():
    f = lax.axis_index("fsdp")
    return lax.axis_index("dp"), f // 8, (f // 2) % NY, f % 2


def device(z, x, y, c):
    return (z, (x * NY + y) * 2 + c)


def gather_kernel(
    prompt_ref, resp_ref, w_ref, gain_hbm, key_gain_hbm, freq_hbm, len_hbm, owner_hbm,
    out_ref,
    gain_ref, key_gain_ref, freq_ref, len_ref, owner_ref,
    hid, normed, wall, wrx, wbuf, acc, meta, meta_rx, cos_ref, sin_ref, cache, picked,
    in_sem, ex_send, ex_recv, n_send, n_recv, up_send, up_recv, down_send, down_recv,
    w2_send, w2_recv, w3_send, w3_recv, w4_send, w4_recv,
    p2_send, p2_recv, p3_send, p3_recv, p4_send, p4_recv,
):
    z, x, y, c = place()
    other = 1 - c

    def to_z(d):
        return device((z + d) % NZ, x, y, c)

    def to_x(d):
        return device(z, (x + d) % NX, y, c)

    def to_y(d):
        return device(z, x, (y + d) % NY, c)

    mate = device(z, x, y, other)

    def copy(src, dst, send, recv, to):
        return pltpu.make_async_remote_copy(
            src_ref=src, dst_ref=dst, send_sem=send, recv_sem=recv, device_id=to, device_id_type=MESH
        )

    in_copies = [
        pltpu.make_async_copy(len_hbm, len_ref, in_sem.at[0]),
        pltpu.make_async_copy(owner_hbm, owner_ref, in_sem.at[1]),
        pltpu.make_async_copy(gain_hbm, gain_ref, in_sem.at[2]),
        pltpu.make_async_copy(key_gain_hbm, key_gain_ref, in_sem.at[3]),
        pltpu.make_async_copy(freq_hbm, freq_ref, in_sem.at[4]),
        pltpu.make_async_copy(prompt_ref, hid.at[pl.ds(0, PG)], in_sem.at[5]),
        pltpu.make_async_copy(resp_ref, hid.at[pl.ds(PG, 8)], in_sem.at[6]),
    ]
    for cp in in_copies:
        cp.start()

    peers = [mate] + [to_z(1), to_z(15)] + [to_x(d) for d in (1, 2, 3)] + [to_y(d) for d in (1, 2, 3)]
    barrier = pltpu.get_barrier_semaphore()
    for peer in peers:
        pl.semaphore_signal(barrier, inc=1, device_id=peer, device_id_type=MESH)

    for kv in range(2):
        for h in range(KVH):
            j = kv * KVH + h
            wall[kv, h] = w_ref[:, j * HD : (j + 1) * HD].astype(jnp.float32)
    in_copies[0].wait()
    in_copies[1].wait()
    owner = owner_ref[0]
    plen = len_ref[owner].astype(jnp.float32)
    line = lax.broadcasted_iota(jnp.int32, (8, HD), 0)
    meta[...] = jnp.where(line == 0, plen, jnp.where(line - 1 == owner, 1.0, 0.0))
    pl.semaphore_wait(barrier, len(peers))

    ex_w = copy(wall.at[:, pl.ds(2 * other, 2)], wrx, ex_send.at[0], ex_recv.at[0], mate)
    ex_w.start()
    ex_m = copy(meta, meta_rx, ex_send.at[1], ex_recv.at[1], mate)
    ex_m.start()
    ex_w.wait_recv()
    for kv in range(2):
        for h in range(2):
            mine = wall[kv, 2 * c + h]
            theirs = wrx[kv, h]
            first = jnp.where(c == 0, mine, theirs)
            second = jnp.where(c == 0, theirs, mine)
            wbuf[z, x, y, 2 * kv + h] = jnp.concatenate([first, second], axis=0).astype(jnp.bfloat16)

    def up_copy(t):
        block = wbuf.at[(z + NZ - t) % NZ, x, y]
        return copy(block, block, up_send.at[t], up_recv.at[t], to_z(1))

    def down_copy(t):
        block = wbuf.at[(z + t) % NZ, x, y]
        return copy(block, block, down_send.at[t], down_recv.at[t], to_z(NZ - 1))

    up_copy(0).start()
    down_copy(0).start()

    for cp in in_copies[2:]:
        cp.wait()
    ex_m.wait_recv()
    freq = freq_ref[...]
    lane = lax.broadcasted_iota(jnp.int32, (32, HD), 1)
    row = lax.broadcasted_iota(jnp.int32, (32, HD), 0)
    sign = jnp.where(lane < HD // 2, -1.0, 1.0)
    mine, theirs = meta[0:1, :], meta_rx[0:1, :]
    lens = (jnp.where(c == 0, mine, theirs), jnp.where(c == 0, theirs, mine))

    @pl.loop(0, 9)
    def _(i):
        j = i - 1
        base = jnp.where(i == 0, (32 * (x * NY + y)).astype(jnp.float32), jnp.where(j < 4, lens[0], lens[1]))
        off = jnp.where(i == 0, 0, (j % 4) * 32)
        angle = (base + (row + off).astype(jnp.float32)) * freq
        cos_ref[i] = jnp.cos(angle)
        sin_ref[i] = jnp.sin(angle) * sign

    acc[...] = jnp.zeros_like(acc)
    gain = gain_ref[...]

    def norm_row(i):
        return jnp.where(i < PG, 2 * i + c, 2 * PG + 8 * c + i - PG)

    def norm_copy(i):
        rows = normed.at[norm_row(i)]
        return copy(rows, rows, n_send.at[i], n_recv.at[i], mate)

    def norm_chunk(i):
        v = hid[i].astype(jnp.float32)
        scale = lax.rsqrt(jnp.mean(v * v, axis=-1, keepdims=True) + EPS)
        normed[norm_row(i)] = (v * scale * gain).astype(jnp.bfloat16)
        norm_copy(i).start()

    def planes(t):
        return (z + t) % NZ, (z + 2 * NZ - 1 - t) % NZ

    def w2_copies(t):
        za, zb = planes(t)
        a, b = wbuf.at[za, x, y], wbuf.at[zb, x, y]
        out = []
        for d in (1, 3, 2):
            out.append(copy(a, a, w2_send.at[t, d - 1], w2_recv.at[t, d - 1], to_y(d)))
            out.append(copy(b, b, w2_send.at[t, d + 2], w2_recv.at[t, d + 2], to_x(d)))
        return out

    def w3_copies(t):
        za, zb = planes(t)
        a, b = wbuf.at[za, x], wbuf.at[zb, :, y]
        return [
            copy(a, a, w3_send.at[t, 0], w3_recv.at[t, 0], to_x(1)),
            copy(b, b, w3_send.at[t, 1], w3_recv.at[t, 1], to_y(1)),
            copy(a, a, w3_send.at[t, 2], w3_recv.at[t, 2], to_x(3)),
            copy(b, b, w3_send.at[t, 3], w3_recv.at[t, 3], to_y(3)),
        ]

    def w4_copies(t):
        za, zb = planes(t)
        lo, hi = pl.ds(0, 2), pl.ds(2, 2)
        a0, b0 = wbuf.at[za, (x + 3) % NX, lo], wbuf.at[zb, lo, (y + 3) % NY]
        a1, b1 = wbuf.at[za, (x + 1) % NX, hi], wbuf.at[zb, hi, (y + 1) % NY]
        return [
            copy(a0, a0, w4_send.at[t, 0], w4_recv.at[t, 0], to_x(1)),
            copy(b0, b0, w4_send.at[t, 1], w4_recv.at[t, 1], to_y(1)),
            copy(a1, a1, w4_send.at[t, 2], w4_recv.at[t, 2], to_x(3)),
            copy(b1, b1, w4_send.at[t, 3], w4_recv.at[t, 3], to_y(3)),
        ]

    @pl.loop(0, 8 + 3 * LAG)
    def _(t):
        @pl.when(jnp.logical_and(t >= 2 * LAG, t < 8 + 2 * LAG))
        def _():
            s = t - 2 * LAG
            for cp in w3_copies(s):
                cp.wait_recv()
            for cp in w4_copies(s):
                cp.start()

        @pl.when(jnp.logical_and(t >= LAG, t < 8 + LAG))
        def _():
            s = t - LAG
            for cp in w2_copies(s):
                cp.wait_recv()
            for cp in w3_copies(s):
                cp.start()

        @pl.when(t < 8)
        def _():
            @pl.when(t >= 1)
            def _():
                down_copy(t - 1).wait_recv()

                @pl.when(t < 7)
                def _():
                    down_copy(t).start()

            up_copy(t).wait_recv()

            @pl.when(t < 7)
            def _():
                up_copy(t + 1).start()

            for cp in w2_copies(t):
                cp.start()

        @pl.when(t < 6)
        def _():
            norm_chunk(2 * t)
            norm_chunk(2 * t + 1)

        @pl.when(t == 3 * LAG)
        def _():
            @pl.loop(0, 12)
            def _(i):
                norm_copy(i).wait_recv()

        @pl.when(t >= 3 * LAG)
        def _():
            s = t - 3 * LAG
            for cp in w4_copies(s):
                cp.wait_recv()
            left, right = [], []
            for plane in planes(s):
                right.append(jnp.concatenate([wbuf[plane, :, :, u].reshape(256, HD) for u in range(4)], axis=1))
                left.append(normed[:, :, pl.ds(pl.multiple_of(plane * 256, 256), 256)].reshape(384, 256))
            left, right = jnp.concatenate(left, axis=1), jnp.concatenate(right, axis=0)
            acc[...] += jnp.dot(left, right, preferred_element_type=jnp.float32)

    key_gain = key_gain_ref[...]

    def finish(kv, h, start, size, cos, sin):
        j = kv * 2 + h
        v = acc[start : start + size, j * HD : (j + 1) * HD]
        if kv == 0:
            v = v * lax.rsqrt(jnp.mean(v * v, axis=-1, keepdims=True) + EPS) * key_gain
            v = v * cos + pltpu.roll(v, HD // 2, 1) * sin
        return v.astype(jnp.bfloat16)

    for h in range(2):
        for kv in range(2):
            for p in range(PG):
                cache[h, p, x, y, kv] = finish(kv, h, p * 32, 32, cos_ref[0], sin_ref[0])

    def p2_copies(p):
        a, b = cache.at[0, p, x, y], cache.at[1, p, x, y]
        out = []
        for d in (1, 3, 2):
            out.append(copy(a, a, p2_send.at[p, d - 1], p2_recv.at[p, d - 1], to_x(d)))
            out.append(copy(b, b, p2_send.at[p, d + 2], p2_recv.at[p, d + 2], to_y(d)))
        return out

    def p3_copies(p):
        a, b = cache.at[0, p, :, y], cache.at[1, p, x]
        return [
            copy(a, a, p3_send.at[p, 0], p3_recv.at[p, 0], to_y(1)),
            copy(b, b, p3_send.at[p, 1], p3_recv.at[p, 1], to_x(1)),
            copy(a, a, p3_send.at[p, 2], p3_recv.at[p, 2], to_y(3)),
            copy(b, b, p3_send.at[p, 3], p3_recv.at[p, 3], to_x(3)),
        ]

    def p4_copies(p):
        lo, hi = pl.ds(0, 2), pl.ds(2, 2)
        a0, b0 = cache.at[0, p, lo, (y + 3) % NY], cache.at[1, p, (x + 3) % NX, lo]
        a1, b1 = cache.at[0, p, hi, (y + 1) % NY], cache.at[1, p, (x + 1) % NX, hi]
        return [
            copy(a0, a0, p4_send.at[p, 0], p4_recv.at[p, 0], to_y(1)),
            copy(b0, b0, p4_send.at[p, 1], p4_recv.at[p, 1], to_x(1)),
            copy(a1, a1, p4_send.at[p, 2], p4_recv.at[p, 2], to_y(3)),
            copy(b1, b1, p4_send.at[p, 3], p4_recv.at[p, 3], to_x(3)),
        ]

    for p in range(PG):
        for cp in p2_copies(p):
            cp.start()

    def resp(kv, h, which):
        cos = cos_ref[pl.ds(1 + 4 * which, 4)].reshape(LR, HD)
        sin = sin_ref[pl.ds(1 + 4 * which, 4)].reshape(LR, HD)
        j = kv * 2 + h
        v = acc[pl.ds(pl.multiple_of(128 + 128 * which, 128), LR), j * HD : (j + 1) * HD]
        if kv == 0:
            v = v * lax.rsqrt(jnp.mean(v * v, axis=-1, keepdims=True) + EPS) * key_gain
            v = v * cos + pltpu.roll(v, HD // 2, 1) * sin
        return v.astype(jnp.bfloat16)

    for h in range(2):
        for kv in range(2):
            picked[kv, h, LP : LP + LR] = resp(kv, h, other)
            out_ref[kv, 2 * c + h, LP : LP + LR] = resp(kv, h, c)
    ex_r = copy(
        picked.at[:, :, pl.ds(LP, LR)], out_ref.at[:, pl.ds(2 * c, 2), pl.ds(LP, LR)],
        ex_send.at[2], ex_recv.at[2], mate,
    )
    ex_r.start()

    @pl.loop(0, PG)
    def _(p):
        for cp in p2_copies(p):
            cp.wait_recv()
        for cp in p3_copies(p):
            cp.start()

    @pl.loop(0, PG)
    def _(p):
        for cp in p3_copies(p):
            cp.wait_recv()
        for cp in p4_copies(p):
            cp.start()

    @pl.loop(0, PG)
    def _(p):
        for cp in p4_copies(p):
            cp.wait_recv()

    ex_o = []
    for h in range(2):
        for kv in range(2):
            total = None
            for p in range(PG):
                weight = meta_rx[1 + p : 2 + p, :].astype(jnp.bfloat16)
                part = cache[h, p, :, :, kv].reshape(LP, HD) * weight
                total = part if total is None else total + part
            picked[kv, h, 0:LP] = total
        cp = copy(
            picked.at[:, h, pl.ds(0, LP)], out_ref.at[:, 2 * c + h, pl.ds(0, LP)],
            ex_send.at[3 + h], ex_recv.at[3 + h], mate,
        )
        cp.start()
        ex_o.append(cp)
    for h in range(2):
        for kv in range(2):
            out_ref[kv, 2 * c + h, 0:LP] = cache[h, owner, :, :, kv].reshape(LP, HD)
    ex_r.wait_recv()
    for cp in ex_o:
        cp.wait_recv()

    ex_w.wait_send()
    ex_m.wait_send()
    ex_r.wait_send()
    for cp in ex_o:
        cp.wait_send()

    @pl.loop(0, 12)
    def _(i):
        norm_copy(i).wait_send()

    up_copy(7).wait_send()

    @pl.loop(0, 7)
    def _(t):
        up_copy(t).wait_send()
        down_copy(t).wait_send()

    @pl.loop(0, 8)
    def _(t):
        for cp in w2_copies(t) + w3_copies(t) + w4_copies(t):
            cp.wait_send()

    @pl.loop(0, PG)
    def _(p):
        for cp in p2_copies(p) + p3_copies(p) + p4_copies(p):
            cp.wait_send()


def attend_kernel(len_ref, owner_ref, rlen_ref, q_ref, kv_ref, o_ref):
    scale = np.float32(np.log2(np.e) / np.sqrt(HD))
    head = pl.program_id(0)

    def columns(g):
        return pl.ds(pl.multiple_of((g * KVH + head) * HD, HD), HD)

    q = jnp.concatenate([q_ref[:, columns(g)] for g in range(QPK)], axis=0)
    keys, vals = kv_ref[0, 0], kv_ref[1, 0]
    s = lax.dot_general(q, keys, (((1,), (1,)), ((), ())), preferred_element_type=jnp.float32) * scale
    plen = len_ref[owner_ref[0]]
    cols = lax.broadcasted_iota(jnp.int32, (LR, LP + LR), 1)
    rows = lax.broadcasted_iota(jnp.int32, (LR, LP + LR), 0)
    allowed = cols < jnp.where(cols < LP, plen, LP + 1 + rows)
    bias = jnp.where(allowed, 0.0, BIG)
    live = lax.broadcasted_iota(jnp.int32, (LR, HD), 0) < rlen_ref[0]
    for g in range(QPK):
        t = s[g * LR : (g + 1) * LR] + bias
        e = jnp.exp2(t - jnp.max(t, axis=-1, keepdims=True))
        total = jnp.sum(e, axis=-1, keepdims=True)
        out = jnp.dot(e.astype(jnp.bfloat16), vals, preferred_element_type=jnp.float32) / total
        o_ref[:, columns(g)] = jnp.where(live, out, 0.0).astype(jnp.bfloat16)


def body(
    prompt_hidden, resp_hidden, resp_query, ln_gain, key_gain, w_kv, prompt_len, resp_len, owner
):
    half = HD // 2
    inv = np.float32(1000000.0) ** (-(np.arange(half, dtype=np.float32) * np.float32(2.0)) / np.float32(HD))
    freq = jnp.asarray(np.concatenate([inv, inv])[None, :].astype(np.float32))
    vmem = pl.BlockSpec(memory_space=pltpu.VMEM)
    smem = pl.BlockSpec(memory_space=pltpu.SMEM)
    anym = pl.BlockSpec(memory_space=pl.ANY)
    bf, f32 = jnp.bfloat16, jnp.float32
    dma = pltpu.SemaphoreType.DMA
    kv = pl.pallas_call(
        gather_kernel,
        name="project_and_share",
        out_shape=jax.ShapeDtypeStruct((2, KVH, LP + LR, HD), bf),
        in_specs=[anym, anym, vmem, anym, anym, anym, anym, anym],
        out_specs=vmem,
        scratch_shapes=[
            pltpu.VMEM((1, D), f32),
            pltpu.VMEM((1, HD), f32),
            pltpu.VMEM((1, HD), f32),
            pltpu.SMEM((PG,), jnp.int32),
            pltpu.SMEM((1,), jnp.int32),
            pltpu.VMEM((12, SUB, D), bf),
            pltpu.VMEM((24, SUB, D), bf),
            pltpu.VMEM((2, KVH, 8, HD), f32),
            pltpu.VMEM((2, 2, 8, HD), f32),
            pltpu.VMEM((NZ, NX, NY, 4, SUB, HD), bf),
            pltpu.VMEM((384, 512), f32),
            pltpu.VMEM((8, HD), f32),
            pltpu.VMEM((8, HD), f32),
            pltpu.VMEM((9, 32, HD), f32),
            pltpu.VMEM((9, 32, HD), f32),
            pltpu.VMEM((2, PG, NX, NY, 2, 32, HD), bf),
            pltpu.VMEM((2, 2, LP + LR, HD), bf),
            dma((7,)), dma((5,)), dma((5,)), dma((12,)), dma((12,)), dma((8,)), dma((8,)), dma((7,)), dma((7,)),
            dma((8, 6)), dma((8, 6)), dma((8, 4)), dma((8, 4)), dma((8, 4)), dma((8, 4)),
            dma((PG, 6)), dma((PG, 6)), dma((PG, 4)), dma((PG, 4)), dma((PG, 4)), dma((PG, 4)),
        ],
        compiler_params=pltpu.CompilerParams(
            collective_id=0, has_side_effects=True, vmem_limit_bytes=62 << 20
        ),
    )(
        prompt_hidden.reshape(PG, SUB, D), resp_hidden.reshape(8, SUB, D), w_kv,
        ln_gain.reshape(1, D), key_gain.reshape(1, HD), freq, prompt_len, owner,
    )
    return pl.pallas_call(
        attend_kernel,
        name="attend",
        out_shape=jax.ShapeDtypeStruct((LR, KVH * QPK * HD), bf),
        grid=(KVH,),
        in_specs=[
            smem, smem, smem,
            pl.BlockSpec((LR, KVH * QPK * HD), lambda h: (0, 0)),
            pl.BlockSpec((2, 1, LP + LR, HD), lambda h: (0, h, 0, 0)),
        ],
        out_specs=pl.BlockSpec((LR, KVH * QPK * HD), lambda h: (0, 0)),
        compiler_params=pltpu.CompilerParams(vmem_limit_bytes=32 << 20),
    )(prompt_len, owner, resp_len, resp_query, kv)


def solution(mesh):
    in_specs = (
        P(("dp", "fsdp"), None),
        P(("dp", "fsdp"), None),
        P(("dp", "fsdp"), None),
        P(),
        P(),
        P(("dp", "fsdp"), None),
        P("dp"),
        P(("dp", "fsdp")),
        P(("dp", "fsdp")),
    )
    out_specs = P(("dp", "fsdp"), None)
    return jax.shard_map(body, mesh=mesh, in_specs=in_specs, out_specs=out_specs, check_vma=False)
```

```python
import functools

import jax
import jax.numpy as jnp
import numpy as np
from jax import lax
from jax.experimental import pallas as pl
from jax.experimental.pallas import tpu as pltpu
from jax.sharding import PartitionSpec as P

MESH = pl.DeviceIdType.MESH
NZ, NX, NY = 16, 4, 4
HD = 128
KVH = 4
QPK = 4
LP = 512
LR = 128
PG = 4
SUB = 16
D = 4096
EPS = 1e-06
BIG = -1e30
LAG = 4
HOP = 3


def place():
    f = lax.axis_index("fsdp")
    return lax.axis_index("dp"), f // 8, (f // 2) % NY, f % 2


def device(z, x, y, c):
    return (z, (x * NY + y) * 2 + c)


def gather_kernel(
    prompt_ref, resp_ref, w_ref, gain_hbm, key_gain_hbm, freq_hbm, len_hbm, owner_hbm,
    out_ref,
    gain_ref, key_gain_ref, freq_ref, len_ref, owner_ref,
    hid, normed, wall, wrx, wbuf, acc, meta, meta_rx, cos_ref, sin_ref, cache, picked,
    in_sem, ex_send, ex_recv, o_send, o_recv, n_send, n_recv, up_send, up_recv, down_send, down_recv,
    w2_send, w2_recv, w3_send, w3_recv, w4_send, w4_recv,
    p2_send, p2_recv, p3_send, p3_recv, p4_send, p4_recv,
):
    z, x, y, c = place()
    other = 1 - c

    def to_z(d):
        return device((z + d) % NZ, x, y, c)

    def to_x(d):
        return device(z, (x + d) % NX, y, c)

    def to_y(d):
        return device(z, x, (y + d) % NY, c)

    mate = device(z, x, y, other)

    def copy(src, dst, send, recv, to):
        return pltpu.make_async_remote_copy(
            src_ref=src, dst_ref=dst, send_sem=send, recv_sem=recv, device_id=to, device_id_type=MESH
        )

    in_copies = [
        pltpu.make_async_copy(len_hbm, len_ref, in_sem.at[0]),
        pltpu.make_async_copy(owner_hbm, owner_ref, in_sem.at[1]),
        pltpu.make_async_copy(gain_hbm, gain_ref, in_sem.at[2]),
        pltpu.make_async_copy(key_gain_hbm, key_gain_ref, in_sem.at[3]),
        pltpu.make_async_copy(freq_hbm, freq_ref, in_sem.at[4]),
        pltpu.make_async_copy(prompt_ref, hid.at[pl.ds(0, PG)], in_sem.at[5]),
        pltpu.make_async_copy(resp_ref, hid.at[pl.ds(PG, 8)], in_sem.at[6]),
    ]
    for cp in in_copies:
        cp.start()

    peers = [mate] + [to_z(d) for k in range(1, HOP + 1) for d in (k, NZ - k)] + [to_x(d) for d in (1, 2, 3)] + [to_y(d) for d in (1, 2, 3)]
    barrier = pltpu.get_barrier_semaphore()
    for peer in peers:
        pl.semaphore_signal(barrier, inc=1, device_id=peer, device_id_type=MESH)

    for kv in range(2):
        for h in range(KVH):
            j = kv * KVH + h
            wall[kv, h] = w_ref[:, j * HD : (j + 1) * HD].astype(jnp.float32)
    in_copies[0].wait()
    in_copies[1].wait()
    owner = owner_ref[0]
    plen = len_ref[owner].astype(jnp.float32)
    line = lax.broadcasted_iota(jnp.int32, (8, HD), 0)
    meta[...] = jnp.where(line == 0, plen, jnp.where(line - 1 == owner, 1.0, 0.0))
    pl.semaphore_wait(barrier, len(peers))

    ex_w = copy(wall.at[:, pl.ds(2 * other, 2)], wrx, ex_send.at[0], ex_recv.at[0], mate)
    ex_w.start()
    ex_m = copy(meta, meta_rx, ex_send.at[1], ex_recv.at[1], mate)
    ex_m.start()
    ex_w.wait_recv()
    for kv in range(2):
        for h in range(2):
            mine = wall[kv, 2 * c + h]
            theirs = wrx[kv, h]
            first = jnp.where(c == 0, mine, theirs)
            second = jnp.where(c == 0, theirs, mine)
            wbuf[z, x, y, 2 * kv + h] = jnp.concatenate([first, second], axis=0).astype(jnp.bfloat16)

    def up_copy(d):
        block = wbuf.at[(z + NZ + HOP - d) % NZ, x, y]
        return copy(block, block, up_send.at[d - 1], up_recv.at[d - 1], to_z(HOP))

    def down_copy(d):
        block = wbuf.at[(z + NZ + d - HOP) % NZ, x, y]
        return copy(block, block, down_send.at[d - 1], down_recv.at[d - 1], to_z(NZ - HOP))

    block = wbuf.at[z, x, y]
    for d in range(1, HOP + 1):
        copy(block, block, up_send.at[d - 1], up_recv.at[d - 1], to_z(d)).start()
        copy(block, block, down_send.at[d - 1], down_recv.at[d - 1], to_z(NZ - d)).start()

    for cp in in_copies[2:]:
        cp.wait()
    ex_m.wait_recv()
    freq = freq_ref[...]
    lane = lax.broadcasted_iota(jnp.int32, (32, HD), 1)
    row = lax.broadcasted_iota(jnp.int32, (32, HD), 0)
    sign = jnp.where(lane < HD // 2, -1.0, 1.0)
    mine, theirs = meta[0:1, :], meta_rx[0:1, :]
    lens = (jnp.where(c == 0, mine, theirs), jnp.where(c == 0, theirs, mine))

    @pl.loop(0, 9)
    def _(i):
        j = i - 1
        base = jnp.where(i == 0, (32 * (x * NY + y)).astype(jnp.float32), jnp.where(j < 4, lens[0], lens[1]))
        off = jnp.where(i == 0, 0, (j % 4) * 32)
        angle = (base + (row + off).astype(jnp.float32)) * freq
        cos_ref[i] = jnp.cos(angle)
        sin_ref[i] = jnp.sin(angle) * sign

    acc[...] = jnp.zeros_like(acc)
    gain = gain_ref[...]

    def norm_row(i):
        return jnp.where(i < PG, 2 * i + c, 2 * PG + 8 * c + i - PG)

    def norm_copy(i):
        rows = normed.at[norm_row(i)]
        return copy(rows, rows, n_send.at[i], n_recv.at[i], mate)

    def norm_chunk(i):
        v = hid[i].astype(jnp.float32)
        scale = lax.rsqrt(jnp.mean(v * v, axis=-1, keepdims=True) + EPS)
        normed[norm_row(i)] = (v * scale * gain).astype(jnp.bfloat16)
        norm_copy(i).start()

    def planes(t):
        return (z + t) % NZ, (z + 2 * NZ - 1 - t) % NZ

    def w2_copies(t):
        za, zb = planes(t)
        a, b = wbuf.at[za, x, y], wbuf.at[zb, x, y]
        out = []
        for d in (1, 3, 2):
            out.append(copy(a, a, w2_send.at[t, d - 1], w2_recv.at[t, d - 1], to_y(d)))
            out.append(copy(b, b, w2_send.at[t, d + 2], w2_recv.at[t, d + 2], to_x(d)))
        return out

    def w3_copies(t):
        za, zb = planes(t)
        a, b = wbuf.at[za, x], wbuf.at[zb, :, y]
        return [
            copy(a, a, w3_send.at[t, 0], w3_recv.at[t, 0], to_x(1)),
            copy(b, b, w3_send.at[t, 1], w3_recv.at[t, 1], to_y(1)),
            copy(a, a, w3_send.at[t, 2], w3_recv.at[t, 2], to_x(3)),
            copy(b, b, w3_send.at[t, 3], w3_recv.at[t, 3], to_y(3)),
        ]

    def w4_copies(t):
        za, zb = planes(t)
        lo, hi = pl.ds(0, 2), pl.ds(2, 2)
        a0, b0 = wbuf.at[za, (x + 3) % NX, lo], wbuf.at[zb, lo, (y + 3) % NY]
        a1, b1 = wbuf.at[za, (x + 1) % NX, hi], wbuf.at[zb, hi, (y + 1) % NY]
        return [
            copy(a0, a0, w4_send.at[t, 0], w4_recv.at[t, 0], to_x(1)),
            copy(b0, b0, w4_send.at[t, 1], w4_recv.at[t, 1], to_y(1)),
            copy(a1, a1, w4_send.at[t, 2], w4_recv.at[t, 2], to_x(3)),
            copy(b1, b1, w4_send.at[t, 3], w4_recv.at[t, 3], to_y(3)),
        ]

    @pl.loop(0, 8 + 3 * LAG)
    def _(t):
        @pl.when(jnp.logical_and(t >= 2 * LAG, t < 8 + 2 * LAG))
        def _():
            s = t - 2 * LAG
            for cp in w3_copies(s):
                cp.wait_recv()
            for cp in w4_copies(s):
                cp.start()

        @pl.when(jnp.logical_and(t >= LAG, t < 8 + LAG))
        def _():
            s = t - LAG
            for cp in w2_copies(s):
                cp.wait_recv()
            for cp in w3_copies(s):
                cp.start()

        @pl.when(t < 8)
        def _():
            @pl.when(t >= 1)
            def _():
                down_copy(t).wait_recv()

                @pl.when(t < 8 - HOP)
                def _():
                    down_copy(t + HOP).start()

            up_copy(t + 1).wait_recv()

            @pl.when(t < 8 - HOP)
            def _():
                up_copy(t + 1 + HOP).start()

            for cp in w2_copies(t):
                cp.start()

        @pl.when(t < 6)
        def _():
            norm_chunk(2 * t)
            norm_chunk(2 * t + 1)

        @pl.when(t == 3 * LAG)
        def _():
            @pl.loop(0, 12)
            def _(i):
                norm_copy(i).wait_recv()

        @pl.when(t >= 3 * LAG)
        def _():
            s = t - 3 * LAG
            for cp in w4_copies(s):
                cp.wait_recv()
            left, right = [], []
            for plane in planes(s):
                right.append(jnp.concatenate([wbuf[plane, :, :, u].reshape(256, HD) for u in range(4)], axis=1))
                left.append(normed[:, :, pl.ds(pl.multiple_of(plane * 256, 256), 256)].reshape(384, 256))
            left, right = jnp.concatenate(left, axis=1), jnp.concatenate(right, axis=0)
            acc[...] += jnp.dot(left, right, preferred_element_type=jnp.float32)

    key_gain = key_gain_ref[...]

    def finish(kv, h, start, size, cos, sin):
        j = kv * 2 + h
        v = acc[start : start + size, j * HD : (j + 1) * HD]
        if kv == 0:
            v = v * lax.rsqrt(jnp.mean(v * v, axis=-1, keepdims=True) + EPS) * key_gain
            v = v * cos + pltpu.roll(v, HD // 2, 1) * sin
        return v.astype(jnp.bfloat16)

    def p2_copies(p):
        a, b = cache.at[0, p, x, y], cache.at[1, p, x, y]
        out = []
        for d in (1, 3, 2):
            out.append(copy(a, a, p2_send.at[p, d - 1], p2_recv.at[p, d - 1], to_x(d)))
            out.append(copy(b, b, p2_send.at[p, d + 2], p2_recv.at[p, d + 2], to_y(d)))
        return out

    def p3_copies(p):
        a, b = cache.at[0, p, :, y], cache.at[1, p, x]
        return [
            copy(a, a, p3_send.at[p, 0], p3_recv.at[p, 0], to_y(1)),
            copy(b, b, p3_send.at[p, 1], p3_recv.at[p, 1], to_x(1)),
            copy(a, a, p3_send.at[p, 2], p3_recv.at[p, 2], to_y(3)),
            copy(b, b, p3_send.at[p, 3], p3_recv.at[p, 3], to_x(3)),
        ]

    def p4_copies(p):
        lo, hi = pl.ds(0, 2), pl.ds(2, 2)
        a0, b0 = cache.at[0, p, lo, (y + 3) % NY], cache.at[1, p, (x + 3) % NX, lo]
        a1, b1 = cache.at[0, p, hi, (y + 1) % NY], cache.at[1, p, (x + 1) % NX, hi]
        return [
            copy(a0, a0, p4_send.at[p, 0], p4_recv.at[p, 0], to_y(1)),
            copy(b0, b0, p4_send.at[p, 1], p4_recv.at[p, 1], to_x(1)),
            copy(a1, a1, p4_send.at[p, 2], p4_recv.at[p, 2], to_y(3)),
            copy(b1, b1, p4_send.at[p, 3], p4_recv.at[p, 3], to_x(3)),
        ]

    for s in range(4):
        kv, cc = s // 2, s % 2
        for h in range(2):
            for p in range(PG):
                cos, sin = cos_ref[0, cc * SUB : (cc + 1) * SUB], sin_ref[0, cc * SUB : (cc + 1) * SUB]
                cache[h, s, x, y, p] = finish(kv, h, p * 32 + cc * SUB, SUB, cos, sin)
        for cp in p2_copies(s):
            cp.start()

    def resp(kv, h, which):
        cos = cos_ref[pl.ds(1 + 4 * which, 4)].reshape(LR, HD)
        sin = sin_ref[pl.ds(1 + 4 * which, 4)].reshape(LR, HD)
        j = kv * 2 + h
        v = acc[pl.ds(pl.multiple_of(128 + 128 * which, 128), LR), j * HD : (j + 1) * HD]
        if kv == 0:
            v = v * lax.rsqrt(jnp.mean(v * v, axis=-1, keepdims=True) + EPS) * key_gain
            v = v * cos + pltpu.roll(v, HD // 2, 1) * sin
        return v.astype(jnp.bfloat16)

    for h in range(2):
        for kv in range(2):
            picked[kv, h, 16:20] = resp(kv, h, other).reshape(4, 2, SUB, HD)
            out_ref[kv, 2 * c + h, 16:20] = resp(kv, h, c).reshape(4, 2, SUB, HD)
    ex_r = copy(
        picked.at[:, :, pl.ds(16, 4)], out_ref.at[:, pl.ds(2 * c, 2), pl.ds(16, 4)],
        ex_send.at[2], ex_recv.at[2], mate,
    )
    ex_r.start()

    @pl.loop(0, PG)
    def _(p):
        for cp in p2_copies(p):
            cp.wait_recv()
        for cp in p3_copies(p):
            cp.start()

    @pl.loop(0, PG)
    def _(p):
        for cp in p3_copies(p):
            cp.wait_recv()
        for cp in p4_copies(p):
            cp.start()

    def ex_copy(s):
        kv, cc = s // 2, s % 2
        return copy(
            picked.at[kv, :, pl.ds(0, 16), cc], out_ref.at[kv, pl.ds(2 * c, 2), pl.ds(0, 16), cc],
            o_send.at[s], o_recv.at[s], mate,
        )

    weights = [meta_rx[1 + p : 2 + p, :].astype(jnp.bfloat16) for p in range(PG)]
    for s in range(4):
        kv, cc = s // 2, s % 2
        for cp in p4_copies(s):
            cp.wait_recv()
        for h in range(2):
            total = None
            for p in range(PG):
                part = cache[h, s, :, :, p].reshape(16, SUB, HD) * weights[p]
                total = part if total is None else total + part
            picked[kv, h, 0:16, cc] = total
        ex_copy(s).start()
    for s in range(4):
        for h in range(2):
            out_ref[s // 2, 2 * c + h, 0:16, s % 2] = cache[h, s, :, :, owner].reshape(16, SUB, HD)
    ex_r.wait_recv()
    for s in range(4):
        ex_copy(s).wait_recv()

    ex_w.wait_send()
    ex_m.wait_send()
    ex_r.wait_send()
    for s in range(4):
        ex_copy(s).wait_send()

    @pl.loop(0, 12)
    def _(i):
        norm_copy(i).wait_send()

    up_copy(8).wait_send()

    @pl.loop(0, 7)
    def _(t):
        up_copy(t + 1).wait_send()
        down_copy(t + 1).wait_send()

    @pl.loop(0, 8)
    def _(t):
        for cp in w2_copies(t) + w3_copies(t) + w4_copies(t):
            cp.wait_send()

    @pl.loop(0, PG)
    def _(p):
        for cp in p2_copies(p) + p3_copies(p) + p4_copies(p):
            cp.wait_send()


def attend_kernel(len_ref, owner_ref, rlen_ref, q_ref, kv_ref, o_ref):
    scale = np.float32(np.log2(np.e) / np.sqrt(HD))
    plen = len_ref[owner_ref[0]]
    cols = lax.broadcasted_iota(jnp.int32, (LR, LP + LR), 1)
    rows = lax.broadcasted_iota(jnp.int32, (LR, LP + LR), 0)
    allowed = cols < jnp.where(cols < LP, plen, LP + 1 + rows)
    bias = jnp.where(allowed, 0.0, BIG)
    live = lax.broadcasted_iota(jnp.int32, (LR, HD), 0) < rlen_ref[0]
    for head in range(KVH):
        keys, vals = kv_ref[0, head], kv_ref[1, head]
        vals = jnp.concatenate([vals, jnp.ones((LP + LR, HD), jnp.bfloat16)], axis=1)
        for g in range(QPK):
            at = (g * KVH + head) * HD
            q = q_ref[:, at : at + HD]
            s = lax.dot_general(q, keys, (((1,), (1,)), ((), ())), preferred_element_type=jnp.float32) * scale
            t = s + bias
            e = jnp.exp2(t - jnp.max(t, axis=-1, keepdims=True))
            out = jnp.dot(e.astype(jnp.bfloat16), vals, preferred_element_type=jnp.float32)
            out = out[:, :HD] / out[:, HD:]
            o_ref[:, at : at + HD] = jnp.where(live, out, 0.0).astype(jnp.bfloat16)


def body(
    prompt_hidden, resp_hidden, resp_query, ln_gain, key_gain, w_kv, prompt_len, resp_len, owner
):
    half = HD // 2
    inv = np.float32(1000000.0) ** (-(np.arange(half, dtype=np.float32) * np.float32(2.0)) / np.float32(HD))
    freq = jnp.asarray(np.concatenate([inv, inv])[None, :].astype(np.float32))
    vmem = pl.BlockSpec(memory_space=pltpu.VMEM)
    smem = pl.BlockSpec(memory_space=pltpu.SMEM)
    anym = pl.BlockSpec(memory_space=pl.ANY)
    bf, f32 = jnp.bfloat16, jnp.float32
    dma = pltpu.SemaphoreType.DMA
    kv = pl.pallas_call(
        gather_kernel,
        name="project_and_share",
        out_shape=jax.ShapeDtypeStruct((2, KVH, 20, 2, SUB, HD), bf),
        in_specs=[anym, anym, vmem, anym, anym, anym, anym, anym],
        out_specs=vmem,
        scratch_shapes=[
            pltpu.VMEM((1, D), f32),
            pltpu.VMEM((1, HD), f32),
            pltpu.VMEM((1, HD), f32),
            pltpu.SMEM((PG,), jnp.int32),
            pltpu.SMEM((1,), jnp.int32),
            pltpu.VMEM((12, SUB, D), bf),
            pltpu.VMEM((24, SUB, D), bf),
            pltpu.VMEM((2, KVH, 8, HD), f32),
            pltpu.VMEM((2, 2, 8, HD), f32),
            pltpu.VMEM((NZ, NX, NY, 4, SUB, HD), bf),
            pltpu.VMEM((384, 512), f32),
            pltpu.VMEM((8, HD), f32),
            pltpu.VMEM((8, HD), f32),
            pltpu.VMEM((9, 32, HD), f32),
            pltpu.VMEM((9, 32, HD), f32),
            pltpu.VMEM((2, 4, NX, NY, PG, SUB, HD), bf),
            pltpu.VMEM((2, 2, 20, 2, SUB, HD), bf),
            dma((7,)), dma((3,)), dma((3,)), dma((4,)), dma((4,)), dma((12,)), dma((12,)), dma((8,)), dma((8,)), dma((7,)), dma((7,)),
            dma((8, 6)), dma((8, 6)), dma((8, 4)), dma((8, 4)), dma((8, 4)), dma((8, 4)),
            dma((PG, 6)), dma((PG, 6)), dma((PG, 4)), dma((PG, 4)), dma((PG, 4)), dma((PG, 4)),
        ],
        compiler_params=pltpu.CompilerParams(
            collective_id=0, has_side_effects=True, vmem_limit_bytes=62 << 20
        ),
    )(
        prompt_hidden.reshape(PG, SUB, D), resp_hidden.reshape(8, SUB, D), w_kv,
        ln_gain.reshape(1, D), key_gain.reshape(1, HD), freq, prompt_len, owner,
    )
    return pl.pallas_call(
        attend_kernel,
        name="attend",
        out_shape=jax.ShapeDtypeStruct((LR, KVH * QPK * HD), bf),
        in_specs=[smem, smem, smem, vmem, vmem],
        out_specs=vmem,
        compiler_params=pltpu.CompilerParams(vmem_limit_bytes=32 << 20),
    )(prompt_len, owner, resp_len, resp_query, kv.reshape(2, KVH, LP + LR, HD))


def solution(mesh):
    in_specs = (
        P(("dp", "fsdp"), None),
        P(("dp", "fsdp"), None),
        P(("dp", "fsdp"), None),
        P(),
        P(),
        P(("dp", "fsdp"), None),
        P("dp"),
        P(("dp", "fsdp")),
        P(("dp", "fsdp")),
    )
    out_specs = P(("dp", "fsdp"), None)
    return jax.shard_map(body, mesh=mesh, in_specs=in_specs, out_specs=out_specs, check_vma=False)
```

```python
import functools

import jax
import jax.numpy as jnp
import numpy as np
from jax import lax
from jax.experimental import pallas as pl
from jax.experimental.pallas import tpu as pltpu
from jax.sharding import PartitionSpec as P

MESH = pl.DeviceIdType.MESH
NZ, NX, NY = 16, 4, 4
HD = 128
KVH = 4
QPK = 4
LP = 512
LR = 128
PG = 4
SUB = 16
D = 4096
EPS = 1e-06
BIG = -1e30
LAG = 4
HOP = 3


def place():
    f = lax.axis_index("fsdp")
    return lax.axis_index("dp"), f // 8, (f // 2) % NY, f % 2


def device(z, x, y, c):
    return (z, (x * NY + y) * 2 + c)


def gather_kernel(
    prompt_ref, resp_ref, w_ref, gain_hbm, key_gain_hbm, freq_hbm, len_hbm, owner_hbm,
    out_ref,
    gain_ref, key_gain_ref, freq_ref, len_ref, owner_ref,
    hid, normed, wall, wrx, wbuf, acc, meta, meta_rx, cos_ref, sin_ref, cache, picked,
    in_sem, ex_send, ex_recv, o_send, o_recv, n_send, n_recv, up_send, up_recv, down_send, down_recv,
    w2_send, w2_recv, w3_send, w3_recv, w4_send, w4_recv,
    p2_send, p2_recv, p3_send, p3_recv, p4_send, p4_recv,
):
    z, x, y, c = place()
    other = 1 - c

    def to_z(d):
        return device((z + d) % NZ, x, y, c)

    def to_x(d):
        return device(z, (x + d) % NX, y, c)

    def to_y(d):
        return device(z, x, (y + d) % NY, c)

    mate = device(z, x, y, other)

    def copy(src, dst, send, recv, to):
        return pltpu.make_async_remote_copy(
            src_ref=src, dst_ref=dst, send_sem=send, recv_sem=recv, device_id=to, device_id_type=MESH
        )

    in_copies = [
        pltpu.make_async_copy(len_hbm, len_ref, in_sem.at[0]),
        pltpu.make_async_copy(owner_hbm, owner_ref, in_sem.at[1]),
        pltpu.make_async_copy(gain_hbm, gain_ref, in_sem.at[2]),
        pltpu.make_async_copy(key_gain_hbm, key_gain_ref, in_sem.at[3]),
        pltpu.make_async_copy(freq_hbm, freq_ref, in_sem.at[4]),
        pltpu.make_async_copy(prompt_ref, hid.at[pl.ds(0, PG)], in_sem.at[5]),
        pltpu.make_async_copy(resp_ref, hid.at[pl.ds(PG, 8)], in_sem.at[6]),
    ]
    for cp in in_copies:
        cp.start()

    peers = [mate] + [to_z(d) for k in range(1, HOP + 1) for d in (k, NZ - k)] + [to_x(d) for d in (1, 2, 3)] + [to_y(d) for d in (1, 2, 3)]
    barrier = pltpu.get_barrier_semaphore()
    for peer in peers:
        pl.semaphore_signal(barrier, inc=1, device_id=peer, device_id_type=MESH)

    for kv in range(2):
        for h in range(KVH):
            j = kv * KVH + h
            wall[kv, h] = w_ref[:, j * HD : (j + 1) * HD].astype(jnp.float32)
    in_copies[0].wait()
    in_copies[1].wait()
    owner = owner_ref[0]
    plen = len_ref[owner].astype(jnp.float32)
    line = lax.broadcasted_iota(jnp.int32, (8, HD), 0)
    meta[...] = jnp.where(line == 0, plen, jnp.where(line - 1 == owner, 1.0, 0.0))
    pl.semaphore_wait(barrier, len(peers))

    ex_w = copy(wall.at[:, pl.ds(2 * other, 2)], wrx, ex_send.at[0], ex_recv.at[0], mate)
    ex_w.start()
    ex_m = copy(meta, meta_rx, ex_send.at[1], ex_recv.at[1], mate)
    ex_m.start()
    ex_w.wait_recv()
    for kv in range(2):
        for h in range(2):
            mine = wall[kv, 2 * c + h]
            theirs = wrx[kv, h]
            first = jnp.where(c == 0, mine, theirs)
            second = jnp.where(c == 0, theirs, mine)
            wbuf[z, x, y, 2 * kv + h] = jnp.concatenate([first, second], axis=0).astype(jnp.bfloat16)

    def up_copy(d):
        block = wbuf.at[(z + NZ + HOP - d) % NZ, x, y]
        return copy(block, block, up_send.at[d - 1], up_recv.at[d - 1], to_z(HOP))

    def down_copy(d):
        block = wbuf.at[(z + NZ + d - HOP) % NZ, x, y]
        return copy(block, block, down_send.at[d - 1], down_recv.at[d - 1], to_z(NZ - HOP))

    block = wbuf.at[z, x, y]
    for d in range(1, HOP + 1):
        copy(block, block, up_send.at[d - 1], up_recv.at[d - 1], to_z(d)).start()
        copy(block, block, down_send.at[d - 1], down_recv.at[d - 1], to_z(NZ - d)).start()

    for cp in in_copies[2:]:
        cp.wait()
    ex_m.wait_recv()
    freq = freq_ref[...]
    lane = lax.broadcasted_iota(jnp.int32, (32, HD), 1)
    row = lax.broadcasted_iota(jnp.int32, (32, HD), 0)
    sign = jnp.where(lane < HD // 2, -1.0, 1.0)
    mine, theirs = meta[0:1, :], meta_rx[0:1, :]
    lens = (jnp.where(c == 0, mine, theirs), jnp.where(c == 0, theirs, mine))

    def angles(i):
        j = i - 1
        base = jnp.where(i == 0, (32 * (x * NY + y)).astype(jnp.float32), jnp.where(j < 4, lens[0], lens[1]))
        off = jnp.where(i == 0, 0, (j % 4) * 32)
        angle = (base + (row + off).astype(jnp.float32)) * freq
        cos_ref[i] = jnp.cos(angle)
        sin_ref[i] = jnp.sin(angle) * sign

    acc[...] = jnp.zeros_like(acc)
    gain = gain_ref[...]

    def norm_row(i):
        return jnp.where(i < PG, 2 * i + c, 2 * PG + 8 * c + i - PG)

    def norm_copy(i):
        rows = normed.at[norm_row(i)]
        return copy(rows, rows, n_send.at[i], n_recv.at[i], mate)

    def norm_chunk(i):
        v = hid[i].astype(jnp.float32)
        scale = lax.rsqrt(jnp.mean(v * v, axis=-1, keepdims=True) + EPS)
        normed[norm_row(i)] = (v * scale * gain).astype(jnp.bfloat16)
        norm_copy(i).start()

    def planes(t):
        return (z + t) % NZ, (z + 2 * NZ - 1 - t) % NZ

    def w2_copies(t):
        za, zb = planes(t)
        a, b = wbuf.at[za, x, y], wbuf.at[zb, x, y]
        out = []
        for d in (1, 3, 2):
            out.append(copy(a, a, w2_send.at[t, d - 1], w2_recv.at[t, d - 1], to_y(d)))
            out.append(copy(b, b, w2_send.at[t, d + 2], w2_recv.at[t, d + 2], to_x(d)))
        return out

    def w3_copies(t):
        za, zb = planes(t)
        a, b = wbuf.at[za, x], wbuf.at[zb, :, y]
        return [
            copy(a, a, w3_send.at[t, 0], w3_recv.at[t, 0], to_x(1)),
            copy(b, b, w3_send.at[t, 1], w3_recv.at[t, 1], to_y(1)),
            copy(a, a, w3_send.at[t, 2], w3_recv.at[t, 2], to_x(3)),
            copy(b, b, w3_send.at[t, 3], w3_recv.at[t, 3], to_y(3)),
        ]

    def w4_copies(t):
        za, zb = planes(t)
        lo, hi = pl.ds(0, 2), pl.ds(2, 2)
        a0, b0 = wbuf.at[za, (x + 3) % NX, lo], wbuf.at[zb, lo, (y + 3) % NY]
        a1, b1 = wbuf.at[za, (x + 1) % NX, hi], wbuf.at[zb, hi, (y + 1) % NY]
        return [
            copy(a0, a0, w4_send.at[t, 0], w4_recv.at[t, 0], to_x(1)),
            copy(b0, b0, w4_send.at[t, 1], w4_recv.at[t, 1], to_y(1)),
            copy(a1, a1, w4_send.at[t, 2], w4_recv.at[t, 2], to_x(3)),
            copy(b1, b1, w4_send.at[t, 3], w4_recv.at[t, 3], to_y(3)),
        ]

    @pl.loop(0, 8 + 3 * LAG)
    def _(t):
        @pl.when(jnp.logical_and(t >= 2 * LAG, t < 8 + 2 * LAG))
        def _():
            s = t - 2 * LAG
            for cp in w3_copies(s):
                cp.wait_recv()
            for cp in w4_copies(s):
                cp.start()

        @pl.when(jnp.logical_and(t >= LAG, t < 8 + LAG))
        def _():
            s = t - LAG
            for cp in w2_copies(s):
                cp.wait_recv()
            for cp in w3_copies(s):
                cp.start()

        @pl.when(t < 8)
        def _():
            @pl.when(t >= 1)
            def _():
                down_copy(t).wait_recv()

                @pl.when(t < 8 - HOP)
                def _():
                    down_copy(t + HOP).start()

            for cp in w2_copies(t)[0::2]:
                cp.start()
            up_copy(t + 1).wait_recv()

            @pl.when(t < 8 - HOP)
            def _():
                up_copy(t + 1 + HOP).start()

            for cp in w2_copies(t)[1::2]:
                cp.start()

        @pl.when(jnp.logical_and(t >= 6, t < 15))
        def _():
            angles(t - 6)

        @pl.when(t < 6)
        def _():
            norm_chunk(2 * t)
            norm_chunk(2 * t + 1)

        @pl.when(t == 3 * LAG)
        def _():
            @pl.loop(0, 12)
            def _(i):
                norm_copy(i).wait_recv()

        @pl.when(t >= 3 * LAG)
        def _():
            s = t - 3 * LAG
            for cp in w4_copies(s):
                cp.wait_recv()
            left, right = [], []
            for plane in planes(s):
                right.append(jnp.concatenate([wbuf[plane, :, :, u].reshape(256, HD) for u in range(4)], axis=1))
                left.append(normed[:, :, pl.ds(pl.multiple_of(plane * 256, 256), 256)].reshape(384, 256))
            left, right = jnp.concatenate(left, axis=1), jnp.concatenate(right, axis=0)
            acc[...] += jnp.dot(left, right, preferred_element_type=jnp.float32)

    key_gain = key_gain_ref[...]

    def finish(kv, h, start, size, cos, sin):
        j = kv * 2 + h
        v = acc[start : start + size, j * HD : (j + 1) * HD]
        if kv == 0:
            v = v * lax.rsqrt(jnp.mean(v * v, axis=-1, keepdims=True) + EPS) * key_gain
            v = v * cos + pltpu.roll(v, HD // 2, 1) * sin
        return v.astype(jnp.bfloat16)

    def p2_copies(p):
        a, b = cache.at[0, p, x, y], cache.at[1, p, x, y]
        out = []
        for d in (1, 3, 2):
            out.append(copy(a, a, p2_send.at[p, d - 1], p2_recv.at[p, d - 1], to_x(d)))
            out.append(copy(b, b, p2_send.at[p, d + 2], p2_recv.at[p, d + 2], to_y(d)))
        return out

    def p3_copies(p):
        a, b = cache.at[0, p, :, y], cache.at[1, p, x]
        return [
            copy(a, a, p3_send.at[p, 0], p3_recv.at[p, 0], to_y(1)),
            copy(b, b, p3_send.at[p, 1], p3_recv.at[p, 1], to_x(1)),
            copy(a, a, p3_send.at[p, 2], p3_recv.at[p, 2], to_y(3)),
            copy(b, b, p3_send.at[p, 3], p3_recv.at[p, 3], to_x(3)),
        ]

    def p4_copies(p):
        lo, hi = pl.ds(0, 2), pl.ds(2, 2)
        a0, b0 = cache.at[0, p, lo, (y + 3) % NY], cache.at[1, p, (x + 3) % NX, lo]
        a1, b1 = cache.at[0, p, hi, (y + 1) % NY], cache.at[1, p, (x + 1) % NX, hi]
        return [
            copy(a0, a0, p4_send.at[p, 0], p4_recv.at[p, 0], to_y(1)),
            copy(b0, b0, p4_send.at[p, 1], p4_recv.at[p, 1], to_x(1)),
            copy(a1, a1, p4_send.at[p, 2], p4_recv.at[p, 2], to_y(3)),
            copy(b1, b1, p4_send.at[p, 3], p4_recv.at[p, 3], to_x(3)),
        ]

    for s in range(4):
        kv, cc = s // 2, s % 2
        for h in range(2):
            for p in range(PG):
                cos, sin = cos_ref[0, cc * SUB : (cc + 1) * SUB], sin_ref[0, cc * SUB : (cc + 1) * SUB]
                cache[h, s, x, y, p] = finish(kv, h, p * 32 + cc * SUB, SUB, cos, sin)
        for cp in p2_copies(s):
            cp.start()

    def resp(kv, h, which):
        cos = cos_ref[pl.ds(1 + 4 * which, 4)].reshape(LR, HD)
        sin = sin_ref[pl.ds(1 + 4 * which, 4)].reshape(LR, HD)
        j = kv * 2 + h
        v = acc[pl.ds(pl.multiple_of(128 + 128 * which, 128), LR), j * HD : (j + 1) * HD]
        if kv == 0:
            v = v * lax.rsqrt(jnp.mean(v * v, axis=-1, keepdims=True) + EPS) * key_gain
            v = v * cos + pltpu.roll(v, HD // 2, 1) * sin
        return v.astype(jnp.bfloat16)

    for h in range(2):
        for kv in range(2):
            picked[kv, h, 16:20] = resp(kv, h, other).reshape(4, 2, SUB, HD)
            out_ref[kv, 2 * c + h, 16:20] = resp(kv, h, c).reshape(4, 2, SUB, HD)
    ex_r = copy(
        picked.at[:, :, pl.ds(16, 4)], out_ref.at[:, pl.ds(2 * c, 2), pl.ds(16, 4)],
        ex_send.at[2], ex_recv.at[2], mate,
    )
    ex_r.start()

    @pl.loop(0, PG)
    def _(p):
        for cp in p2_copies(p):
            cp.wait_recv()
        for cp in p3_copies(p):
            cp.start()

    @pl.loop(0, PG)
    def _(p):
        for cp in p3_copies(p):
            cp.wait_recv()
        for cp in p4_copies(p):
            cp.start()

    def ex_copy(s):
        kv, cc = s // 2, s % 2
        return copy(
            picked.at[kv, :, pl.ds(0, 16), cc], out_ref.at[kv, pl.ds(2 * c, 2), pl.ds(0, 16), cc],
            o_send.at[s], o_recv.at[s], mate,
        )

    weights = [meta_rx[1 + p : 2 + p, :].astype(jnp.bfloat16) for p in range(PG)]
    for s in range(4):
        kv, cc = s // 2, s % 2
        for cp in p4_copies(s):
            cp.wait_recv()
        for h in range(2):
            total = None
            for p in range(PG):
                part = cache[h, s, :, :, p].reshape(16, SUB, HD) * weights[p]
                total = part if total is None else total + part
            picked[kv, h, 0:16, cc] = total
        ex_copy(s).start()
    for s in range(4):
        for h in range(2):
            out_ref[s // 2, 2 * c + h, 0:16, s % 2] = cache[h, s, :, :, owner].reshape(16, SUB, HD)
    ex_r.wait_recv()
    for s in range(4):
        ex_copy(s).wait_recv()

    ex_w.wait_send()
    ex_m.wait_send()
    ex_r.wait_send()
    for s in range(4):
        ex_copy(s).wait_send()

    @pl.loop(0, 12)
    def _(i):
        norm_copy(i).wait_send()

    up_copy(8).wait_send()

    @pl.loop(0, 7)
    def _(t):
        up_copy(t + 1).wait_send()
        down_copy(t + 1).wait_send()

    @pl.loop(0, 8)
    def _(t):
        for cp in w2_copies(t) + w3_copies(t) + w4_copies(t):
            cp.wait_send()

    @pl.loop(0, PG)
    def _(p):
        for cp in p2_copies(p) + p3_copies(p) + p4_copies(p):
            cp.wait_send()


def attend_kernel(len_ref, owner_ref, rlen_ref, q_ref, kv_ref, o_ref):
    scale = np.float32(np.log2(np.e) / np.sqrt(HD))
    plen = len_ref[owner_ref[0]]
    cols = lax.broadcasted_iota(jnp.int32, (LR, LP + LR), 1)
    rows = lax.broadcasted_iota(jnp.int32, (LR, LP + LR), 0)
    allowed = cols < jnp.where(cols < LP, plen, LP + 1 + rows)
    bias = jnp.where(allowed, 0.0, BIG)
    live = lax.broadcasted_iota(jnp.int32, (LR, HD), 0) < rlen_ref[0]
    for head in range(KVH):
        keys, vals = kv_ref[0, head], kv_ref[1, head]
        vals = jnp.concatenate([vals, jnp.ones((LP + LR, HD), jnp.bfloat16)], axis=1)
        for g in range(QPK):
            at = (g * KVH + head) * HD
            q = q_ref[:, at : at + HD]
            s = lax.dot_general(q, keys, (((1,), (1,)), ((), ())), preferred_element_type=jnp.float32) * scale
            t = s + bias
            e = jnp.exp2(t - jnp.max(t, axis=-1, keepdims=True))
            out = jnp.dot(e.astype(jnp.bfloat16), vals, preferred_element_type=jnp.float32)
            out = out[:, :HD] / out[:, HD:]
            o_ref[:, at : at + HD] = jnp.where(live, out, 0.0).astype(jnp.bfloat16)


def body(
    prompt_hidden, resp_hidden, resp_query, ln_gain, key_gain, w_kv, prompt_len, resp_len, owner
):
    half = HD // 2
    inv = np.float32(1000000.0) ** (-(np.arange(half, dtype=np.float32) * np.float32(2.0)) / np.float32(HD))
    freq = jnp.asarray(np.concatenate([inv, inv])[None, :].astype(np.float32))
    vmem = pl.BlockSpec(memory_space=pltpu.VMEM)
    smem = pl.BlockSpec(memory_space=pltpu.SMEM)
    anym = pl.BlockSpec(memory_space=pl.ANY)
    bf, f32 = jnp.bfloat16, jnp.float32
    dma = pltpu.SemaphoreType.DMA
    kv = pl.pallas_call(
        gather_kernel,
        name="project_and_share",
        out_shape=jax.ShapeDtypeStruct((2, KVH, 20, 2, SUB, HD), bf),
        in_specs=[anym, anym, vmem, anym, anym, anym, anym, anym],
        out_specs=vmem,
        scratch_shapes=[
            pltpu.VMEM((1, D), f32),
            pltpu.VMEM((1, HD), f32),
            pltpu.VMEM((1, HD), f32),
            pltpu.SMEM((PG,), jnp.int32),
            pltpu.SMEM((1,), jnp.int32),
            pltpu.VMEM((12, SUB, D), bf),
            pltpu.VMEM((24, SUB, D), bf),
            pltpu.VMEM((2, KVH, 8, HD), f32),
            pltpu.VMEM((2, 2, 8, HD), f32),
            pltpu.VMEM((NZ, NX, NY, 4, SUB, HD), bf),
            pltpu.VMEM((384, 512), f32),
            pltpu.VMEM((8, HD), f32),
            pltpu.VMEM((8, HD), f32),
            pltpu.VMEM((9, 32, HD), f32),
            pltpu.VMEM((9, 32, HD), f32),
            pltpu.VMEM((2, 4, NX, NY, PG, SUB, HD), bf),
            pltpu.VMEM((2, 2, 20, 2, SUB, HD), bf),
            dma((7,)), dma((3,)), dma((3,)), dma((4,)), dma((4,)), dma((12,)), dma((12,)), dma((8,)), dma((8,)), dma((7,)), dma((7,)),
            dma((8, 6)), dma((8, 6)), dma((8, 4)), dma((8, 4)), dma((8, 4)), dma((8, 4)),
            dma((PG, 6)), dma((PG, 6)), dma((PG, 4)), dma((PG, 4)), dma((PG, 4)), dma((PG, 4)),
        ],
        compiler_params=pltpu.CompilerParams(
            collective_id=0, has_side_effects=True, vmem_limit_bytes=62 << 20
        ),
    )(
        prompt_hidden.reshape(PG, SUB, D), resp_hidden.reshape(8, SUB, D), w_kv,
        ln_gain.reshape(1, D), key_gain.reshape(1, HD), freq, prompt_len, owner,
    )
    return pl.pallas_call(
        attend_kernel,
        name="attend",
        out_shape=jax.ShapeDtypeStruct((LR, KVH * QPK * HD), bf),
        in_specs=[smem, smem, smem, vmem, vmem],
        out_specs=vmem,
        compiler_params=pltpu.CompilerParams(vmem_limit_bytes=32 << 20),
    )(prompt_len, owner, resp_len, resp_query, kv.reshape(2, KVH, LP + LR, HD))


def solution(mesh):
    in_specs = (
        P(("dp", "fsdp"), None),
        P(("dp", "fsdp"), None),
        P(("dp", "fsdp"), None),
        P(),
        P(),
        P(("dp", "fsdp"), None),
        P("dp"),
        P(("dp", "fsdp")),
        P(("dp", "fsdp")),
    )
    out_specs = P(("dp", "fsdp"), None)
    return jax.shard_map(body, mesh=mesh, in_specs=in_specs, out_specs=out_specs, check_vma=False)
```
